512 devices in a mesh: dp: 8 (over y), node: 8 (over x, core), local: 8 (over z).
Axes of the slice: x: 4, y: 8, z: 8, core: 2. Of those that a mesh axis runs over, the one named last changes fastest.
Arguments:
- tokens: bfloat16 [4096, 3584], P(('dp', 'node', 'local')), may hold values from -6 to 6
- grad_out: bfloat16 [4096, 3584], P(('dp', 'node', 'local')), may hold values from -6 to 6
- router_gates: bfloat16 [4096, 4], P(('dp', 'node', 'local')), may hold values from 0.19921875 to 1
- groups: int32 [4096, 4], P(('dp', 'node', 'local')), may hold values from 0 to 7, all different within a row; in each aligned block of 8 rows (0 to 7, 8 to 15, ...) at most 6 rows name the same one
- w_gate: bfloat16 [8, 3584, 1024], P('node', 'dp', 'local'), may hold values from -0.09375 to 0.09375
- w_up: bfloat16 [8, 3584, 1024], P('node', 'dp', 'local'), may hold values from -0.09375 to 0.09375
- w_down: bfloat16 [8, 1024, 3584], P('node', 'local', 'dp'), may hold values from -0.1875 to 0.1875
Outputs:
- grad_tokens: bfloat16 [4096, 3584], P(('dp', 'node', 'local'))
- grad_gates: bfloat16 [4096, 4], P(('dp', 'node', 'local'))
- grad_gate: bfloat16 [8, 3584, 1024], P('node', None, 'local')
- grad_up: bfloat16 [8, 3584, 1024], P('node', None, 'local')
- grad_down: bfloat16 [8, 1024, 3584], P('node', 'local')
The draws below stay inside these ranges and needn't reach their ends.
Inputs may be any that keep to these rules, and one draw needn't show every extreme that they name: Each token names 4 different node groups. Among the 8 tokens of one device no group is named by more than 6 tokens, a bound that some block reaches.
All inputs are finite; a program needn't handle non-finite values.
Results may differ from the reference program's by a relative error of at most 0.017.
Values may be sent and summed in bfloat16 or wider, within the bound.
No kernel may reach another device: no remote copies, remote signals or barrier semaphores. Data moves between devices by JAX's collectives and lax.ppermute only.
A program may use at most 64 MiB of HBM per device.

```python
import math
import jax
import jax.numpy as jnp
import numpy as np
from jax import lax

D = 3584
HID = 1024
TOK_DEV = 8
TOP = 4
CAP = 6
TOKENS = 4096
N_DP = 8
N_NODE = 8
N_LOCAL = 8


def block_levels(stream_key, extent, shards, least, largest):
    level, own = 1.0, jax.random.fold_in(stream_key, 6)
    for dim, shards_of in shards:
        heights = jnp.exp(jax.random.uniform(jax.random.fold_in(own, dim), (shards_of,), jnp.float32, least / len(shards), largest / len(shards)))
        level = level * jnp.repeat(heights, extent[dim] // shards_of).reshape([-1 if axis == dim else 1 for axis in range(len(extent))])
    return level


def deal_out(key, own, number, rows, number_of, top, limit, skew):
    ranking = jax.random.permutation(key, number_of)
    heavy_load, common = shares(number_of, rows * top, limit, skew, True), shares(number_of, rows * top, limit, skew, False)
    places = jnp.arange(number_of)

    def named(sizes, turn):
        used = int((sizes > 0).sum())
        fixed = max(1, used // 4)
        moved = fixed + (places - fixed + turn * (used - fixed)) % max(1, number_of - fixed)
        return jnp.zeros((number_of,), jnp.int32).at[ranking[jnp.where(places < fixed, places, moved)]].set(jnp.asarray(sizes, jnp.int32))

    sizes = jnp.where(number % 4 == 0, named(heavy_load, number // 4), named(common, number - number // 4 - 1))
    mixed = jax.random.permutation(jax.random.fold_in(own, 3), number_of)
    giver, sink = mixed[0:number_of // 2 * 2:2], mixed[1:number_of // 2 * 2:2]
    room = jnp.minimum(sizes[giver] - 1, limit - sizes[sink]) // 2
    room = jnp.where((giver == ranking[0]) | (sink == ranking[0]) | (sizes[sink] == 0), 0, jnp.maximum(room, 0))
    moved = jax.random.randint(jax.random.fold_in(own, 4), (number_of // 2,), 0, 1 << 20) % (room + 1)
    sizes = sizes.at[giver].add(-moved).at[sink].add(moved)
    items = jnp.searchsorted(jnp.cumsum(sizes), jnp.arange(rows * top), side="right").astype(jnp.int32)
    grid = items.reshape(top, rows).T
    grid = grid[jax.random.permutation(jax.random.fold_in(own, 1), rows)]
    turn = jax.random.randint(jax.random.fold_in(own, 2), (rows, 1), 0, top)
    return jnp.take_along_axis(grid, (jnp.arange(top)[None, :] + turn) % top, axis=1)


def shares(number_of, total, reach, slope, full):
    loads = [(1 << 20) // math.isqrt(standing ** slope) + 1 for standing in range(1, number_of + 1)]
    largest = reach if full else min(reach, max(-(-total // number_of), total * loads[0] // sum(loads)))
    least = 1 if total - largest >= number_of - 1 else 0
    counts, rest = [largest] + [least] * (number_of - 1), total - largest - least * (number_of - 1)
    while rest > 0:
        candidates = [i for i in range(1, number_of) if counts[i] < largest] or [i for i in range(1, number_of) if counts[i] < reach]
        pool, left = sum([loads[i] for i in candidates]), rest
        for i in candidates:
            more = min(reach - counts[i], max(1, left * loads[i] // pool), rest)
            counts[i] = counts[i] + more
            rest = rest - more
    return np.array(counts)


def normal_values(key, dims, deviation, limit, shards=(), kind=jnp.bfloat16):
    values = deviation * jax.random.normal(key, dims, jnp.float32)
    if shards:
        values = values * block_levels(key, dims, shards, -0.22, 0.18)
    return jnp.clip(values, -limit, limit).astype(kind)


def setup_inputs(seed: int = 0) -> dict:
    key_list = jax.random.split(jax.random.key(seed), 8)
    tokens = normal_values(key_list[0], (TOKENS, D), 1.0, 6.0, ((0, 512),))
    grad_out = normal_values(key_list[1], (TOKENS, D), 1.0, 6.0, ((0, 512),))
    router_gates = jnp.clip(0.19921875 + 0.80078125 * jax.random.uniform(key_list[2], (TOKENS, TOP), jnp.float32) ** block_levels(key_list[2], (TOKENS, TOP), ((0, 512),), -0.2, 0.2), 0.19921875, 1.0).astype(jnp.bfloat16)
    groups_keys = jax.random.split(jax.random.fold_in(key_list[3], 1), TOKENS // TOK_DEV)
    groups_turns = jax.random.permutation(jax.random.fold_in(key_list[3], 3), TOKENS // TOK_DEV)
    groups = jax.vmap(lambda own, number: deal_out(jax.random.fold_in(key_list[3], 2), own, number, TOK_DEV, N_NODE, TOP, CAP, 2))(groups_keys, groups_turns).reshape((TOKENS, TOP))
    w_gate = normal_values(key_list[4], (N_NODE, D, HID), D ** -0.5, 0.09375, ((0, 8), (1, 8), (2, 8)))
    w_up = normal_values(key_list[5], (N_NODE, D, HID), D ** -0.5, 0.09375, ((0, 8), (1, 8), (2, 8)))
    w_down = normal_values(key_list[6], (N_NODE, HID, D), HID ** -0.5, 0.1875, ((0, 8), (1, 8), (2, 8)))
    return dict(tokens=tokens, grad_out=grad_out, router_gates=router_gates, groups=groups, w_gate=w_gate, w_up=w_up, w_down=w_down)


def rounded(value):
    return lax.optimization_barrier(value.astype(jnp.bfloat16)).astype(jnp.float32)


def reference(tokens, grad_out, router_gates, groups, w_gate, w_up, w_down):
    dp_rows = TOKENS // N_DP
    hidden_shard = HID // N_LOCAL

    def per_expert(expert):
        gate_mat = w_gate[expert]
        up_mat = w_up[expert]
        down_mat = w_down[expert]
        gate_split = gate_mat.astype(jnp.float32).reshape(D, N_LOCAL, hidden_shard)
        up_split = up_mat.astype(jnp.float32).reshape(D, N_LOCAL, hidden_shard)
        down_split = down_mat.astype(jnp.float32).reshape(N_LOCAL, hidden_shard, D)

        def per_replica(totals, replica):
            start = (replica * dp_rows).astype(jnp.int32)
            inputs = lax.dynamic_slice_in_dim(tokens, start, dp_rows, 0)
            upstream = lax.dynamic_slice_in_dim(grad_out, start, dp_rows, 0)
            weights = lax.dynamic_slice_in_dim(router_gates, start, dp_rows, 0)
            choice_ids = lax.dynamic_slice_in_dim(groups, start, dp_rows, 0)
            weight = jnp.sum(jnp.where(choice_ids == expert, weights.astype(jnp.float32), jnp.float32(0.0)), axis=1)
            pre_gate = jnp.dot(inputs, gate_mat, preferred_element_type=jnp.float32)
            pre_up = jnp.dot(inputs, up_mat, preferred_element_type=jnp.float32)
            sigmoid_gate = jax.nn.sigmoid(pre_gate)
            activated = (pre_gate * sigmoid_gate * pre_up).astype(jnp.bfloat16)
            scaled = (weight[:, None] * upstream.astype(jnp.float32)).astype(jnp.bfloat16)
            shard_out = jnp.einsum("rlh,lhd->rld", activated.astype(jnp.float32).reshape(dp_rows, N_LOCAL, hidden_shard), down_split)
            gate_part = jnp.sum(upstream.astype(jnp.float32)[:, None, :] * shard_out, axis=2)
            expert_gate = jnp.sum(rounded(gate_part), axis=1).astype(jnp.bfloat16)
            grad_act = jnp.dot(scaled, down_mat.T, preferred_element_type=jnp.float32)
            gate_back = (grad_act * pre_up * sigmoid_gate * (1.0 + pre_gate * (1.0 - sigmoid_gate))).astype(jnp.bfloat16)
            up_back = (grad_act * pre_gate * sigmoid_gate).astype(jnp.bfloat16)
            input_part = jnp.einsum("rlh,dlh->rld", gate_back.astype(jnp.float32).reshape(dp_rows, N_LOCAL, hidden_shard), gate_split)
            input_part = input_part + jnp.einsum("rlh,dlh->rld", up_back.astype(jnp.float32).reshape(dp_rows, N_LOCAL, hidden_shard), up_split)
            expert_input = jnp.sum(rounded(input_part), axis=1).astype(jnp.bfloat16)
            term_gate = jnp.dot(inputs.T, gate_back, preferred_element_type=jnp.float32)
            term_up = jnp.dot(inputs.T, up_back, preferred_element_type=jnp.float32)
            term_down = jnp.dot(activated.T, scaled, preferred_element_type=jnp.float32)
            totals = (totals[0] + rounded(term_gate), totals[1] + rounded(term_up), totals[2] + rounded(term_down))
            return totals, (expert_input, expert_gate)

        start_totals = (jnp.zeros((D, HID), jnp.float32), jnp.zeros((D, HID), jnp.float32), jnp.zeros((HID, D), jnp.float32))
        totals, (inputs_all, gates_all) = lax.scan(per_replica, start_totals, jnp.arange(N_DP).astype(jnp.int32))
        return (totals[0].astype(jnp.bfloat16), totals[1].astype(jnp.bfloat16), totals[2].astype(jnp.bfloat16), inputs_all, gates_all)

    grad_gate, grad_up, grad_down, inputs_all, gates_all = lax.map(per_expert, jnp.arange(N_NODE).astype(jnp.int32))
    grad_tokens = jnp.sum(inputs_all.reshape(N_NODE, TOKENS, D).astype(jnp.float32), axis=0).astype(jnp.bfloat16)
    expert_ids = jnp.arange(N_NODE).astype(jnp.int32)
    onehot = (groups[None, :, :] == expert_ids[:, None, None]).astype(jnp.float32)
    per_token = gates_all.reshape(N_NODE, TOKENS).astype(jnp.float32)
    grad_gates = jnp.sum(onehot * per_token[:, :, None], axis=0).astype(jnp.bfloat16)
    return grad_tokens, grad_gates, grad_gate, grad_up, grad_down
```

```python
import functools

import jax
import jax.numpy as jnp
from jax import lax
from jax.experimental import pallas as pl
from jax.experimental.pallas import tpu as pltpu
from jax.sharding import PartitionSpec as P

LANES = 128
STEP = 512


def gradients_kernel(n_own, n_other, z_ref, sel_ref, w_hbm, *refs):
    own = refs[:n_own]
    other = refs[n_own : n_own + n_other]
    grads_ref, back_ref, part_ref, rows, weights, sems = refs[n_own + n_other :]
    half = rows.shape[0] // 2
    width = (rows.shape[1] - LANES) // 2
    block = own[0].shape[0]
    places = half // block
    here = z_ref[0]
    copies = [pltpu.make_async_copy(w_hbm, weights, sems.at[0])]
    offsets = ring_offsets(places)
    count = 0
    for base, group in ((0, own), (half, other)):
        index = 0
        for ref in group:
            for piece in range(ref.shape[0] // block):
                slot = lax.rem(here + (offsets[index] + places), places)
                start = pl.multiple_of(base + slot * block, block)
                copies.append(
                    pltpu.make_async_copy(
                        ref.at[pl.ds(piece * block, block)],
                        rows.at[pl.ds(start, block)],
                        sems.at[1 + count],
                    )
                )
                index += 1
                count += 1
    for copy in copies:
        copy.start()
    for copy in copies:
        copy.wait()

    def project(step, total):
        span = pl.ds(pl.multiple_of(step * STEP, STEP), STEP)
        return total + jnp.dot(
            rows[:, span], weights[span, : 2 * LANES], preferred_element_type=jnp.float32
        )

    def project_back(step, total):
        span = pl.ds(pl.multiple_of(step * STEP, STEP), STEP)
        shifted = pl.ds(pl.multiple_of(width + step * STEP, STEP), STEP)
        return total + jnp.dot(
            rows[:, shifted], weights[span, 2 * LANES :], preferred_element_type=jnp.float32
        )

    steps = width // STEP
    pre = lax.fori_loop(0, steps, project, jnp.zeros((2 * half, 2 * LANES), jnp.float32))
    raw = lax.fori_loop(0, steps, project_back, jnp.zeros((2 * half, LANES), jnp.float32))
    pre_gate, pre_up = pre[:, :LANES], pre[:, LANES:]
    sel = sel_ref[0:1, :]
    weight = jnp.sum(rows[:, 2 * width :].astype(jnp.float32) * sel, axis=1, keepdims=True)
    sigmoid = jax.nn.sigmoid(pre_gate)
    activated = (pre_gate * sigmoid * pre_up).astype(jnp.bfloat16).astype(jnp.float32)
    part_ref[...] = (jnp.sum(activated * raw, axis=1, keepdims=True) * sel).astype(jnp.bfloat16)
    grad_act = raw * weight
    back_gate = grad_act * pre_up * sigmoid * (1.0 + pre_gate * (1.0 - sigmoid))
    back_up = grad_act * pre_gate * sigmoid
    back = jnp.concatenate([back_gate, back_up], axis=1)
    back_ref[...] = back.astype(jnp.bfloat16)
    back_t = back.T.astype(jnp.bfloat16)
    activated_t = (activated * weight).T.astype(jnp.bfloat16)

    def terms(step, carry):
        span = pl.ds(pl.multiple_of(step * STEP, STEP), STEP)
        shifted = pl.ds(pl.multiple_of(width + step * STEP, STEP), STEP)
        grads_ref[: 2 * LANES, span] = jnp.dot(
            back_t, rows[:, span], preferred_element_type=jnp.float32
        ).astype(jnp.bfloat16)
        grads_ref[2 * LANES :, span] = jnp.dot(
            activated_t, rows[:, shifted], preferred_element_type=jnp.float32
        ).astype(jnp.bfloat16)
        return carry

    lax.fori_loop(0, steps, terms, 0)


def input_kernel(back_ref, part_ref, w_ref, own_ref, other_ref):
    half = own_ref.shape[0]
    width = own_ref.shape[1] - LANES

    def step_of(step, carry):
        span = pl.ds(pl.multiple_of(step * STEP, STEP), STEP)
        out = lax.dot_general(
            back_ref[...],
            w_ref[span, : 2 * LANES],
            (((1,), (1,)), ((), ())),
            preferred_element_type=jnp.float32,
        ).astype(jnp.bfloat16)
        own_ref[:, span] = out[:half]
        other_ref[:, span] = out[half:]
        return carry

    lax.fori_loop(0, width // STEP, step_of, 0)
    own_ref[:, width:] = part_ref[:half]
    other_ref[:, width:] = part_ref[half:]


def unpack_kernel(sum_ref, gate_ref, up_ref, down_ref):
    gate_ref[0] = sum_ref[:LANES, :].astype(jnp.float32).T.astype(jnp.bfloat16)
    up_ref[0] = sum_ref[LANES : 2 * LANES, :].astype(jnp.float32).T.astype(jnp.bfloat16)
    down_ref[0] = sum_ref[2 * LANES :, :]


def ring_offsets(places):
    offsets = [0]
    for hop in range(1, places // 2 + 1):
        offsets.append(-hop)
        if hop < places - hop:
            offsets.append(hop)
    return offsets


def params():
    return pltpu.CompilerParams(vmem_limit_bytes=48 * 1024 * 1024)


def shards(tokens, grad_out, router_gates, groups, w_gate, w_up, w_down):
    nodes = lax.axis_size("node")
    places = lax.axis_size("local")
    count, width = tokens.shape
    columns = nodes // 2
    node = lax.axis_index("node")
    place = lax.axis_index("local")
    wide = 2 * width + LANES

    lanes = jnp.arange(LANES, dtype=jnp.int32)
    hits = groups[:, :, None] == lanes[None, None, :]
    table = jnp.sum(
        jnp.where(hits, router_gates.astype(jnp.float32)[:, :, None], 0.0), axis=1
    ).astype(jnp.bfloat16)
    mine = jnp.concatenate([tokens, grad_out, table], axis=1)
    packed = jnp.concatenate([w_gate[0], w_up[0], w_down[0].T], axis=1)
    weights = lax.all_gather(packed, "dp", axis=0, tiled=True)

    same_core = [[2 * x + core for x in range(columns)] for core in range(2)]
    block = lax.all_gather(mine, "node", axis=0, tiled=True, axis_index_groups=same_core)
    up = [(i, (i + 1) % places) for i in range(places)]
    down = [(i, (i - 1) % places) for i in range(places)]
    cores = [(i, i ^ 1) for i in range(nodes)]
    rising = falling = block
    own = [block]
    for hop in range(1, places // 2 + 1):
        rising = lax.ppermute(rising, "local", up)
        own.append(rising)
        if hop < places - hop:
            falling = lax.ppermute(falling, "local", down)
            own.append(falling)
    other = [
        lax.ppermute(jnp.concatenate(own[a:b], axis=0), "node", cores)
        for a, b in ((0, 3), (3, 5), (5, len(own)))
    ]

    half = places * columns * count
    sel = jnp.broadcast_to((lanes == node).astype(jnp.float32)[None], (8, LANES))
    vmem = pl.BlockSpec(memory_space=pltpu.VMEM)
    anywhere = pl.BlockSpec(memory_space=pl.ANY)
    grads, back, part = pl.pallas_call(
        functools.partial(gradients_kernel, len(own), len(other)),
        out_shape=(
            jax.ShapeDtypeStruct((3 * LANES, width), jnp.bfloat16),
            jax.ShapeDtypeStruct((2 * half, 2 * LANES), jnp.bfloat16),
            jax.ShapeDtypeStruct((2 * half, LANES), jnp.bfloat16),
        ),
        in_specs=[pl.BlockSpec(memory_space=pltpu.SMEM), vmem]
        + [anywhere] * (1 + len(own) + len(other)),
        out_specs=(vmem, vmem, vmem),
        scratch_shapes=[
            pltpu.VMEM((2 * half, wide), jnp.bfloat16),
            pltpu.VMEM((width, 3 * LANES), jnp.bfloat16),
            pltpu.SemaphoreType.DMA((1 + 2 * places,)),
        ],
        compiler_params=params(),
        name="gradients",
    )(place.astype(jnp.int32)[None], sel, weights, *own, *other)

    summed = lax.psum(grads, "dp")

    part_own, part_other = pl.pallas_call(
        input_kernel,
        out_shape=(
            jax.ShapeDtypeStruct((half, width + LANES), jnp.bfloat16),
            jax.ShapeDtypeStruct((half, width + LANES), jnp.bfloat16),
        ),
        in_specs=[vmem, vmem, vmem],
        out_specs=(vmem, vmem),
        compiler_params=params(),
        name="input_part",
    )(back, part, weights)
    arrived = lax.ppermute(part_other, "node", cores)
    chip = (part_own.astype(jnp.float32) + arrived.astype(jnp.float32)).astype(jnp.bfloat16)
    by_place = lax.all_to_all(
        chip.reshape(places, columns * count, width + LANES), "local", 0, 0, tiled=True
    )
    column = jnp.sum(by_place.astype(jnp.float32), axis=0).astype(jnp.bfloat16)
    by_column = lax.all_to_all(
        column.reshape(columns, count, width + LANES),
        "node",
        0,
        0,
        tiled=True,
        axis_index_groups=same_core,
    )
    total = jnp.sum(by_column.astype(jnp.float32), axis=0)
    grad_tokens = total[:, :width].astype(jnp.bfloat16)
    grad_gates = jnp.sum(jnp.where(hits, total[:, None, width:], 0.0), axis=2).astype(jnp.bfloat16)

    grad_gate, grad_up, grad_down = pl.pallas_call(
        unpack_kernel,
        out_shape=(
            jax.ShapeDtypeStruct((1, width, LANES), jnp.bfloat16),
            jax.ShapeDtypeStruct((1, width, LANES), jnp.bfloat16),
            jax.ShapeDtypeStruct((1, LANES, width), jnp.bfloat16),
        ),
        in_specs=[vmem],
        out_specs=(vmem, vmem, vmem),
        compiler_params=params(),
        name="unpack",
    )(summed)
    return grad_tokens, grad_gates, grad_gate, grad_up, grad_down


def solution(mesh):
    placed = (
        P(("dp", "node", "local"), None),
        P(("dp", "node", "local"), None),
        P(("dp", "node", "local"), None),
        P(("dp", "node", "local"), None),
        P("node", "dp", "local"),
        P("node", "dp", "local"),
        P("node", "local", "dp"),
    )
    return jax.shard_map(
        shards,
        mesh=mesh,
        in_specs=placed,
        out_specs=(
            P(("dp", "node", "local"), None),
            P(("dp", "node", "local"), None),
            P("node", None, "local"),
            P("node", None, "local"),
            P("node", "local", None),
        ),
        check_vma=False,
    )
```

```python
import functools

import jax
import jax.numpy as jnp
from jax import lax
from jax.experimental import pallas as pl
from jax.experimental.pallas import tpu as pltpu
from jax.sharding import PartitionSpec as P

LANES = 128
STEP = 1792


def gradients_kernel(plan, z_ref, sel_ref, w_hbm, *refs):
    blocks = refs[: len(plan)]
    grads_hbm, back_ref, part_ref, rows, weights, grads, sems = refs[len(plan) :]
    half = rows.shape[0] // 2
    width = (rows.shape[1] - LANES) // 2
    here, towards = z_ref[0], z_ref[1]
    size = blocks[0].shape[0]
    places = half // size
    early = [pltpu.make_async_copy(w_hbm, weights, sems.at[0])]
    late = []
    for source, (hop, which) in zip(blocks, plan):
        slot = lax.rem(here + towards * hop + places, places)
        target = rows.at[pl.ds(pl.multiple_of(which * half + slot * size, size), size)]
        count = len(early)
        for group, first, columns in ((early, 0, width), (late, width, width + LANES)):
            group.append(
                pltpu.make_async_copy(
                    source.at[:, pl.ds(first, columns)],
                    target.at[:, pl.ds(first, columns)],
                    sems.at[count + (2 * places if first else 0)],
                )
            )
    for copy in early + late:
        copy.start()
    for copy in early:
        copy.wait()

    def project(step, total):
        span = pl.ds(pl.multiple_of(step * STEP, STEP), STEP)
        return total + jnp.dot(
            rows[:, span], weights[span, : 2 * LANES], preferred_element_type=jnp.float32
        )

    def project_back(step, total):
        span = pl.ds(pl.multiple_of(step * STEP, STEP), STEP)
        shifted = pl.ds(pl.multiple_of(width + step * STEP, STEP), STEP)
        return total + jnp.dot(
            rows[:, shifted], weights[span, 2 * LANES :], preferred_element_type=jnp.float32
        )

    steps = width // STEP
    pre = lax.fori_loop(0, steps, project, jnp.zeros((2 * half, 2 * LANES), jnp.float32))
    for copy in late:
        copy.wait()
    raw = lax.fori_loop(0, steps, project_back, jnp.zeros((2 * half, LANES), jnp.float32))
    pre_gate, pre_up = pre[:, :LANES], pre[:, LANES:]
    sel = sel_ref[0:1, :]
    weight = jnp.sum(rows[:, 2 * width :].astype(jnp.float32) * sel, axis=1, keepdims=True)
    sigmoid = jax.nn.sigmoid(pre_gate)
    activated = (pre_gate * sigmoid * pre_up).astype(jnp.bfloat16).astype(jnp.float32)
    part_ref[...] = (jnp.sum(activated * raw, axis=1, keepdims=True) * sel).astype(jnp.bfloat16)
    grad_act = raw * weight
    back_gate = grad_act * pre_up * sigmoid * (1.0 + pre_gate * (1.0 - sigmoid))
    back_up = grad_act * pre_gate * sigmoid
    back = jnp.concatenate([back_gate, back_up], axis=1)
    back_ref[...] = back.astype(jnp.bfloat16)
    back_t = back.T.astype(jnp.bfloat16)
    activated_t = (activated * weight).T.astype(jnp.bfloat16)

    outgoing = []
    for step in range(steps):
        span = pl.ds(step * STEP, STEP)
        grads[: 2 * LANES, span] = jnp.dot(
            back_t, rows[:, span], preferred_element_type=jnp.float32
        ).astype(jnp.bfloat16)
        grads[2 * LANES :, span] = jnp.dot(
            activated_t,
            rows[:, pl.ds(width + step * STEP, STEP)],
            preferred_element_type=jnp.float32,
        ).astype(jnp.bfloat16)
        outgoing.append(
            pltpu.make_async_copy(
                grads.at[:, span], grads_hbm.at[:, span], sems.at[4 * places + 1 + step]
            )
        )
        outgoing[-1].start()
    for copy in outgoing:
        copy.wait()


def input_kernel(back_ref, part_ref, w_ref, own_ref, other_ref):
    half = own_ref.shape[0]
    width = own_ref.shape[1] - LANES

    def step_of(step, carry):
        span = pl.ds(pl.multiple_of(step * STEP, STEP), STEP)
        out = lax.dot_general(
            back_ref[...],
            w_ref[span, : 2 * LANES],
            (((1,), (1,)), ((), ())),
            preferred_element_type=jnp.float32,
        ).astype(jnp.bfloat16)
        own_ref[:, span] = out[:half]
        other_ref[:, span] = out[half:]
        return carry

    lax.fori_loop(0, width // STEP, step_of, 0)
    own_ref[:, width:] = part_ref[:half]
    other_ref[:, width:] = part_ref[half:]


def unpack_kernel(sum_ref, gate_ref, up_ref, down_ref):
    gate_ref[0] = sum_ref[:LANES, :].astype(jnp.float32).T.astype(jnp.bfloat16)
    up_ref[0] = sum_ref[LANES : 2 * LANES, :].astype(jnp.float32).T.astype(jnp.bfloat16)
    down_ref[0] = sum_ref[2 * LANES :, :]


def params():
    return pltpu.CompilerParams(vmem_limit_bytes=48 * 1024 * 1024)


def shards(tokens, grad_out, router_gates, groups, w_gate, w_up, w_down):
    nodes = lax.axis_size("node")
    places = lax.axis_size("local")
    count, width = tokens.shape
    columns = nodes // 2
    node = lax.axis_index("node")
    place = lax.axis_index("local")
    wide = 2 * width + LANES

    lanes = jnp.arange(LANES, dtype=jnp.int32)
    hits = groups[:, :, None] == lanes[None, None, :]
    table = jnp.sum(
        jnp.where(hits, router_gates.astype(jnp.float32)[:, :, None], 0.0), axis=1
    ).astype(jnp.bfloat16)
    mine = jnp.concatenate([tokens, grad_out, table], axis=1)
    packed = jnp.concatenate([w_gate[0], w_up[0], w_down[0].T], axis=1)
    weights = lax.all_gather(packed, "dp", axis=0, tiled=True)

    same_core = [[2 * x + core for x in range(columns)] for core in range(2)]
    block = lax.all_gather(mine, "node", axis=0, tiled=True, axis_index_groups=same_core)
    cores = [(i, i ^ 1) for i in range(nodes)]
    ring = [
        (n * places + z, n * places + (z + 1 - 2 * (n % 2)) % places)
        for n in range(nodes)
        for z in range(places)
    ]
    swap = lambda piece: lax.ppermute(piece, "node", cores)
    chains = [block, swap(block)]
    blocks, plan = list(chains), [(0, 0), (0, 1)]
    for hop in range(1, places // 2 + 1):
        for which in range(1 if 2 * hop == places else 2):
            chains[which] = lax.ppermute(chains[which], ("node", "local"), ring)
            blocks += [chains[which], swap(chains[which])]
            plan += [(hop, which), (-hop, 1 - which)]

    half = places * block.shape[0]
    core = lax.rem(node, 2)
    where = jnp.stack([place, 2 * core - 1]).astype(jnp.int32)
    sel = jnp.broadcast_to((lanes == node).astype(jnp.float32)[None], (8, LANES))
    vmem = pl.BlockSpec(memory_space=pltpu.VMEM)
    anywhere = pl.BlockSpec(memory_space=pl.ANY)
    grads, back, part = pl.pallas_call(
        functools.partial(gradients_kernel, plan),
        out_shape=(
            jax.ShapeDtypeStruct((3 * LANES, width), jnp.bfloat16),
            jax.ShapeDtypeStruct((2 * half, 2 * LANES), jnp.bfloat16),
            jax.ShapeDtypeStruct((2 * half, LANES), jnp.bfloat16),
        ),
        in_specs=[pl.BlockSpec(memory_space=pltpu.SMEM), vmem] + [anywhere] * (1 + len(blocks)),
        out_specs=(anywhere, vmem, vmem),
        scratch_shapes=[
            pltpu.VMEM((2 * half, wide), jnp.bfloat16),
            pltpu.VMEM((width, 3 * LANES), jnp.bfloat16),
            pltpu.VMEM((3 * LANES, width), jnp.bfloat16),
            pltpu.SemaphoreType.DMA((4 * places + 1 + width // STEP,)),
        ],
        compiler_params=params(),
        name="gradients",
    )(where, sel, weights, *blocks)

    share = lax.psum_scatter(grads, "dp", scatter_dimension=0, tiled=True)

    part_own, part_other = pl.pallas_call(
        input_kernel,
        out_shape=(
            jax.ShapeDtypeStruct((half, width + LANES), jnp.bfloat16),
            jax.ShapeDtypeStruct((half, width + LANES), jnp.bfloat16),
        ),
        in_specs=[vmem, vmem, vmem],
        out_specs=(vmem, vmem),
        compiler_params=params(),
        name="input_part",
    )(back, part, weights)
    arrived = lax.ppermute(part_other, "node", cores)
    chip = (part_own.astype(jnp.float32) + arrived.astype(jnp.float32)).astype(jnp.bfloat16)
    chip = chip.reshape(places, columns * count, width + LANES)
    cut = width // 2
    first = lax.all_to_all(chip[:, :, :cut], "local", 0, 0, tiled=True)
    share, first, rest = lax.optimization_barrier((share, first, chip[:, :, cut:]))
    summed = lax.all_gather(share, "dp", axis=0, tiled=True)
    rest = lax.all_to_all(rest, "local", 0, 0, tiled=True)
    column = jnp.concatenate(
        [jnp.sum(part.astype(jnp.float32), axis=0).astype(jnp.bfloat16) for part in (first, rest)],
        axis=1,
    )
    by_column = lax.all_to_all(
        column.reshape(columns, count, width + LANES),
        "node",
        0,
        0,
        tiled=True,
        axis_index_groups=same_core,
    )
    total = jnp.sum(by_column.astype(jnp.float32), axis=0)
    grad_tokens = total[:, :width].astype(jnp.bfloat16)
    grad_gates = jnp.sum(jnp.where(hits, total[:, None, width:], 0.0), axis=2).astype(jnp.bfloat16)

    grad_gate, grad_up, grad_down = pl.pallas_call(
        unpack_kernel,
        out_shape=(
            jax.ShapeDtypeStruct((1, width, LANES), jnp.bfloat16),
            jax.ShapeDtypeStruct((1, width, LANES), jnp.bfloat16),
            jax.ShapeDtypeStruct((1, LANES, width), jnp.bfloat16),
        ),
        in_specs=[vmem],
        out_specs=(vmem, vmem, vmem),
        compiler_params=params(),
        name="unpack",
    )(summed)
    return grad_tokens, grad_gates, grad_gate, grad_up, grad_down


def solution(mesh):
    placed = (
        P(("dp", "node", "local"), None),
        P(("dp", "node", "local"), None),
        P(("dp", "node", "local"), None),
        P(("dp", "node", "local"), None),
        P("node", "dp", "local"),
        P("node", "dp", "local"),
        P("node", "local", "dp"),
    )
    return jax.shard_map(
        shards,
        mesh=mesh,
        in_specs=placed,
        out_specs=(
            P(("dp", "node", "local"), None),
            P(("dp", "node", "local"), None),
            P("node", None, "local"),
            P("node", None, "local"),
            P("node", "local", None),
        ),
        check_vma=False,
    )
```

```python
import functools

import jax
import jax.numpy as jnp
from jax import lax
from jax.experimental import pallas as pl
from jax.experimental.pallas import tpu as pltpu
from jax.sharding import PartitionSpec as P

LANES = 128
STEP = 1792


def gradients_kernel(plan, z_ref, sel_ref, w_hbm, *refs):
    blocks = refs[: len(plan)]
    grads_hbm, back_ref, part_ref, rows, weights, grads, sems = refs[len(plan) :]
    half = rows.shape[0] // 2
    width = (rows.shape[1] - LANES) // 2
    here, towards = z_ref[0], z_ref[1]
    size = blocks[0].shape[0]
    places = half // size
    early = [pltpu.make_async_copy(w_hbm, weights, sems.at[0])]
    late = []
    for source, (hop, which) in zip(blocks, plan):
        slot = lax.rem(here + towards * hop + places, places)
        target = rows.at[pl.ds(pl.multiple_of(which * half + slot * size, size), size)]
        count = len(early)
        for group, first, columns in ((early, 0, width), (late, width, width + LANES)):
            group.append(
                pltpu.make_async_copy(
                    source.at[:, pl.ds(first, columns)],
                    target.at[:, pl.ds(first, columns)],
                    sems.at[count + (2 * places if first else 0)],
                )
            )
    for copy in early + late:
        copy.start()
    for copy in early:
        copy.wait()

    def project(step, total):
        span = pl.ds(pl.multiple_of(step * STEP, STEP), STEP)
        return total + jnp.dot(
            rows[:, span], weights[span, : 2 * LANES], preferred_element_type=jnp.float32
        )

    def project_back(step, total):
        span = pl.ds(pl.multiple_of(step * STEP, STEP), STEP)
        shifted = pl.ds(pl.multiple_of(width + step * STEP, STEP), STEP)
        return total + jnp.dot(
            rows[:, shifted], weights[span, 2 * LANES :], preferred_element_type=jnp.float32
        )

    steps = width // STEP
    pre = lax.fori_loop(0, steps, project, jnp.zeros((2 * half, 2 * LANES), jnp.float32))
    for copy in late:
        copy.wait()
    raw = lax.fori_loop(0, steps, project_back, jnp.zeros((2 * half, LANES), jnp.float32))
    pre_gate, pre_up = pre[:, :LANES], pre[:, LANES:]
    sel = sel_ref[0:1, :]
    weight = jnp.sum(rows[:, 2 * width :].astype(jnp.float32) * sel, axis=1, keepdims=True)
    sigmoid = jax.nn.sigmoid(pre_gate)
    activated = (pre_gate * sigmoid * pre_up).astype(jnp.bfloat16).astype(jnp.float32)
    part_ref[...] = (jnp.sum(activated * raw, axis=1, keepdims=True) * sel).astype(jnp.bfloat16)
    grad_act = raw * weight
    back_gate = grad_act * pre_up * sigmoid * (1.0 + pre_gate * (1.0 - sigmoid))
    back_up = grad_act * pre_gate * sigmoid
    back = jnp.concatenate([back_gate, back_up], axis=1)
    back_ref[...] = back.astype(jnp.bfloat16)
    back_t = back.T.astype(jnp.bfloat16)
    activated_t = (activated * weight).T.astype(jnp.bfloat16)

    outgoing = []
    for step in range(steps):
        span = pl.ds(step * STEP, STEP)
        grads[: 2 * LANES, span] = jnp.dot(
            back_t, rows[:, span], preferred_element_type=jnp.float32
        ).astype(jnp.bfloat16)
        grads[2 * LANES :, span] = jnp.dot(
            activated_t,
            rows[:, pl.ds(width + step * STEP, STEP)],
            preferred_element_type=jnp.float32,
        ).astype(jnp.bfloat16)
        outgoing.append(
            pltpu.make_async_copy(
                grads.at[:, span], grads_hbm.at[:, span], sems.at[4 * places + 1 + step]
            )
        )
        outgoing[-1].start()
    for copy in outgoing:
        copy.wait()


def input_kernel(back_ref, part_ref, w_ref, own_ref, other_ref):
    half = own_ref.shape[0]
    width = own_ref.shape[1] - LANES

    def step_of(step, carry):
        span = pl.ds(pl.multiple_of(step * STEP, STEP), STEP)
        out = lax.dot_general(
            back_ref[...],
            w_ref[span, : 2 * LANES],
            (((1,), (1,)), ((), ())),
            preferred_element_type=jnp.float32,
        ).astype(jnp.bfloat16)
        own_ref[:, span] = out[:half]
        other_ref[:, span] = out[half:]
        return carry

    lax.fori_loop(0, width // STEP, step_of, 0)
    own_ref[:, width:] = part_ref[:half]
    other_ref[:, width:] = part_ref[half:]


def unpack_kernel(sum_hbm, gate_hbm, up_hbm, down_hbm, held, turned, sems):
    pieces = [pl.ds(n * LANES, LANES) for n in range(3)]
    arrivals = [
        pltpu.make_async_copy(sum_hbm.at[piece], held.at[piece], sems.at[n])
        for n, piece in enumerate(pieces)
    ]
    for copy in arrivals:
        copy.start()
    leaving = []
    for n, target in enumerate((gate_hbm, up_hbm)):
        arrivals[n].wait()
        turned[n] = held[pieces[n], :].astype(jnp.float32).T.astype(jnp.bfloat16)
        leaving.append(pltpu.make_async_copy(turned.at[n], target.at[0], sems.at[3 + n]))
        leaving[-1].start()
    arrivals[2].wait()
    leaving.append(pltpu.make_async_copy(held.at[pieces[2]], down_hbm.at[0], sems.at[5]))
    leaving[-1].start()
    for copy in leaving:
        copy.wait()


def params():
    return pltpu.CompilerParams(vmem_limit_bytes=60 * 1024 * 1024)


def shards(tokens, grad_out, router_gates, groups, w_gate, w_up, w_down):
    nodes = lax.axis_size("node")
    places = lax.axis_size("local")
    count, width = tokens.shape
    columns = nodes // 2
    node = lax.axis_index("node")
    place = lax.axis_index("local")
    wide = 2 * width + LANES

    lanes = jnp.arange(LANES, dtype=jnp.int32)
    hits = groups[:, :, None] == lanes[None, None, :]
    table = jnp.sum(
        jnp.where(hits, router_gates.astype(jnp.float32)[:, :, None], 0.0), axis=1
    ).astype(jnp.bfloat16)
    mine = jnp.concatenate([tokens, grad_out, table], axis=1)
    same_core = [[2 * x + core for x in range(columns)] for core in range(2)]
    block = lax.all_to_all(
        jnp.broadcast_to(mine, (columns, count, wide)),
        "node",
        0,
        0,
        tiled=True,
        axis_index_groups=same_core,
    ).reshape(columns * count, wide)
    block, gate, up, down = lax.optimization_barrier((block, w_gate[0], w_up[0], w_down[0]))
    packed = jnp.concatenate([gate, up, down.T], axis=1)
    weights = lax.all_gather(packed, "dp", axis=0, tiled=True)
    cores = [(i, i ^ 1) for i in range(nodes)]
    ring = [
        (n * places + z, n * places + (z + 1 - 2 * (n % 2)) % places)
        for n in range(nodes)
        for z in range(places)
    ]
    swap = lambda piece: lax.ppermute(piece, "node", cores)
    chains = list(lax.optimization_barrier((block, swap(block))))
    blocks, plan = list(chains), [(0, 0), (0, 1)]
    for hop in range(1, places // 2 + 1):
        for which in range(1 if 2 * hop == places else 2):
            chains[which] = lax.ppermute(chains[which], ("node", "local"), ring)
            blocks += [chains[which], swap(chains[which])]
            plan += [(hop, which), (-hop, 1 - which)]

    half = places * block.shape[0]
    core = lax.rem(node, 2)
    where = jnp.stack([place, 2 * core - 1]).astype(jnp.int32)
    sel = jnp.broadcast_to((lanes == node).astype(jnp.float32)[None], (8, LANES))
    vmem = pl.BlockSpec(memory_space=pltpu.VMEM)
    anywhere = pl.BlockSpec(memory_space=pl.ANY)
    grads, back, part = pl.pallas_call(
        functools.partial(gradients_kernel, plan),
        out_shape=(
            jax.ShapeDtypeStruct((3 * LANES, width), jnp.bfloat16),
            jax.ShapeDtypeStruct((2 * half, 2 * LANES), jnp.bfloat16),
            jax.ShapeDtypeStruct((2 * half, LANES), jnp.bfloat16),
        ),
        in_specs=[pl.BlockSpec(memory_space=pltpu.SMEM), vmem] + [anywhere] * (1 + len(blocks)),
        out_specs=(anywhere, vmem, vmem),
        scratch_shapes=[
            pltpu.VMEM((2 * half, wide), jnp.bfloat16),
            pltpu.VMEM((width, 3 * LANES), jnp.bfloat16),
            pltpu.VMEM((3 * LANES, width), jnp.bfloat16),
            pltpu.SemaphoreType.DMA((4 * places + 1 + width // STEP,)),
        ],
        compiler_params=params(),
        name="gradients",
    )(where, sel, weights, *blocks)

    share = lax.psum_scatter(grads, "dp", scatter_dimension=0, tiled=True)

    part_own, part_other = pl.pallas_call(
        input_kernel,
        out_shape=(
            jax.ShapeDtypeStruct((half, width + LANES), jnp.bfloat16),
            jax.ShapeDtypeStruct((half, width + LANES), jnp.bfloat16),
        ),
        in_specs=[vmem, vmem, vmem],
        out_specs=(vmem, vmem),
        compiler_params=params(),
        name="input_part",
    )(back, part, weights)
    arrived = lax.ppermute(part_other, "node", cores)
    chip = (part_own.astype(jnp.float32) + arrived.astype(jnp.float32)).astype(jnp.bfloat16)
    chip = chip.reshape(places, columns * count, width + LANES)
    cut = width // 2
    first = lax.all_to_all(chip[:, :, :cut], "local", 0, 0, tiled=True)
    share, first, rest = lax.optimization_barrier((share, first, chip[:, :, cut:]))
    summed = lax.all_gather(share, "dp", axis=0, tiled=True)
    rest = lax.all_to_all(rest, "local", 0, 0, tiled=True)
    column = jnp.concatenate(
        [jnp.sum(part.astype(jnp.float32), axis=0).astype(jnp.bfloat16) for part in (first, rest)],
        axis=1,
    )
    by_column = lax.all_to_all(
        column.reshape(columns, count, width + LANES),
        "node",
        0,
        0,
        tiled=True,
        axis_index_groups=same_core,
    )
    total = jnp.sum(by_column.astype(jnp.float32), axis=0)
    grad_tokens = total[:, :width].astype(jnp.bfloat16)
    grad_gates = jnp.sum(jnp.where(hits, total[:, None, width:], 0.0), axis=2).astype(jnp.bfloat16)

    grad_gate, grad_up, grad_down = pl.pallas_call(
        unpack_kernel,
        out_shape=(
            jax.ShapeDtypeStruct((1, width, LANES), jnp.bfloat16),
            jax.ShapeDtypeStruct((1, width, LANES), jnp.bfloat16),
            jax.ShapeDtypeStruct((1, LANES, width), jnp.bfloat16),
        ),
        in_specs=[anywhere],
        out_specs=(anywhere, anywhere, anywhere),
        scratch_shapes=[
            pltpu.VMEM((3 * LANES, width), jnp.bfloat16),
            pltpu.VMEM((2, width, LANES), jnp.bfloat16),
            pltpu.SemaphoreType.DMA((6,)),
        ],
        compiler_params=params(),
        name="unpack",
    )(summed)
    return grad_tokens, grad_gates, grad_gate, grad_up, grad_down


def solution(mesh):
    placed = (
        P(("dp", "node", "local"), None),
        P(("dp", "node", "local"), None),
        P(("dp", "node", "local"), None),
        P(("dp", "node", "local"), None),
        P("node", "dp", "local"),
        P("node", "dp", "local"),
        P("node", "local", "dp"),
    )
    return jax.shard_map(
        shards,
        mesh=mesh,
        in_specs=placed,
        out_specs=(
            P(("dp", "node", "local"), None),
            P(("dp", "node", "local"), None),
            P("node", None, "local"),
            P("node", None, "local"),
            P("node", "local", None),
        ),
        check_vma=False,
    )
```

```python
import functools

import jax
import jax.numpy as jnp
from jax import lax
from jax.experimental import pallas as pl
from jax.experimental.pallas import tpu as pltpu
from jax.sharding import PartitionSpec as P

LANES = 128
STEP = 1792


def gradients_kernel(plan, w_hbm, *refs):
    blocks = refs[: len(plan)]
    grads_hbm, back_ref, part_ref, rows, weights, grads, sems = refs[len(plan) :]
    half = rows.shape[0] // 2
    width = (rows.shape[1] - LANES) // 2
    node = lax.axis_index("node")
    here, towards = lax.axis_index("local"), 2 * lax.rem(node, 2) - 1
    size = blocks[0].shape[0]
    places = half // size
    early = [pltpu.make_async_copy(w_hbm, weights, sems.at[0])]
    late = []
    for source, (hop, which) in zip(blocks, plan):
        slot = lax.rem(here + towards * hop + places, places)
        target = rows.at[pl.ds(pl.multiple_of(which * half + slot * size, size), size)]
        count = len(early)
        for group, first, columns in ((early, 0, width), (late, width, width + LANES)):
            group.append(
                pltpu.make_async_copy(
                    source.at[:, pl.ds(first, columns)],
                    target.at[:, pl.ds(first, columns)],
                    sems.at[count + (2 * places if first else 0)],
                )
            )
    for copy in early + late:
        copy.start()
    for copy in early:
        copy.wait()

    def project(step, total):
        span = pl.ds(pl.multiple_of(step * STEP, STEP), STEP)
        return total + jnp.dot(
            rows[:, span], weights[span, : 2 * LANES], preferred_element_type=jnp.float32
        )

    def project_back(step, total):
        span = pl.ds(pl.multiple_of(step * STEP, STEP), STEP)
        shifted = pl.ds(pl.multiple_of(width + step * STEP, STEP), STEP)
        return total + jnp.dot(
            rows[:, shifted], weights[span, 2 * LANES :], preferred_element_type=jnp.float32
        )

    steps = width // STEP
    pre = lax.fori_loop(0, steps, project, jnp.zeros((2 * half, 2 * LANES), jnp.float32))
    for copy in late:
        copy.wait()
    raw = lax.fori_loop(0, steps, project_back, jnp.zeros((2 * half, LANES), jnp.float32))
    pre_gate, pre_up = pre[:, :LANES], pre[:, LANES:]
    lanes = lax.broadcasted_iota(jnp.int32, (1, LANES), 1)
    sel = (lanes == node).astype(jnp.float32)
    weight = jnp.sum(rows[:, 2 * width :].astype(jnp.float32) * sel, axis=1, keepdims=True)
    sigmoid = jax.nn.sigmoid(pre_gate)
    activated = (pre_gate * sigmoid * pre_up).astype(jnp.bfloat16).astype(jnp.float32)
    part_ref[...] = (jnp.sum(activated * raw, axis=1, keepdims=True) * sel).astype(jnp.bfloat16)
    grad_act = raw * weight
    back_gate = grad_act * pre_up * sigmoid * (1.0 + pre_gate * (1.0 - sigmoid))
    back_up = grad_act * pre_gate * sigmoid
    back = jnp.concatenate([back_gate, back_up], axis=1)
    back_ref[...] = back.astype(jnp.bfloat16)
    back_t = back.T.astype(jnp.bfloat16)
    activated_t = (activated * weight).T.astype(jnp.bfloat16)

    outgoing = []
    for step in range(steps):
        span = pl.ds(step * STEP, STEP)
        grads[: 2 * LANES, span] = jnp.dot(
            back_t, rows[:, span], preferred_element_type=jnp.float32
        ).astype(jnp.bfloat16)
        grads[2 * LANES :, span] = jnp.dot(
            activated_t,
            rows[:, pl.ds(width + step * STEP, STEP)],
            preferred_element_type=jnp.float32,
        ).astype(jnp.bfloat16)
        outgoing.append(
            pltpu.make_async_copy(
                grads.at[:, span], grads_hbm.at[:, span], sems.at[4 * places + 1 + step]
            )
        )
        outgoing[-1].start()
    for copy in outgoing:
        copy.wait()


def input_kernel(back_ref, part_ref, w_ref, own_ref, other_ref):
    half = own_ref.shape[0]
    width = own_ref.shape[1] - LANES

    def step_of(step, carry):
        span = pl.ds(pl.multiple_of(step * STEP, STEP), STEP)
        out = lax.dot_general(
            back_ref[...],
            w_ref[span, : 2 * LANES],
            (((1,), (1,)), ((), ())),
            preferred_element_type=jnp.float32,
        ).astype(jnp.bfloat16)
        own_ref[:, span] = out[:half]
        other_ref[:, span] = out[half:]
        return carry

    lax.fori_loop(0, width // STEP, step_of, 0)
    own_ref[:, width:] = part_ref[:half]
    other_ref[:, width:] = part_ref[half:]


def unpack_kernel(sum_hbm, gate_hbm, up_hbm, down_hbm, held, turned, sems):
    pieces = [pl.ds(n * LANES, LANES) for n in range(3)]
    arrivals = [
        pltpu.make_async_copy(sum_hbm.at[piece], held.at[piece], sems.at[n])
        for n, piece in enumerate(pieces)
    ]
    for copy in arrivals:
        copy.start()
    leaving = []
    for n, target in enumerate((gate_hbm, up_hbm)):
        arrivals[n].wait()
        turned[n] = held[pieces[n], :].astype(jnp.float32).T.astype(jnp.bfloat16)
        leaving.append(pltpu.make_async_copy(turned.at[n], target.at[0], sems.at[3 + n]))
        leaving[-1].start()
    arrivals[2].wait()
    leaving.append(pltpu.make_async_copy(held.at[pieces[2]], down_hbm.at[0], sems.at[5]))
    leaving[-1].start()
    for copy in leaving:
        copy.wait()


def params():
    return pltpu.CompilerParams(vmem_limit_bytes=60 * 1024 * 1024)


def shards(tokens, grad_out, router_gates, groups, w_gate, w_up, w_down):
    nodes = lax.axis_size("node")
    places = lax.axis_size("local")
    count, width = tokens.shape
    columns = nodes // 2
    wide = 2 * width + LANES

    lanes = jnp.arange(LANES, dtype=jnp.int32)
    hits = groups[:, :, None] == lanes[None, None, :]
    table = jnp.sum(
        jnp.where(hits, router_gates.astype(jnp.float32)[:, :, None], 0.0), axis=1
    ).astype(jnp.bfloat16)
    mine = jnp.concatenate([tokens, grad_out, table], axis=1)
    same_core = [[2 * x + core for x in range(columns)] for core in range(2)]
    block = lax.all_to_all(
        jnp.broadcast_to(mine, (columns, count, wide)),
        "node",
        0,
        0,
        tiled=True,
        axis_index_groups=same_core,
    ).reshape(columns * count, wide)
    block, gate, up, down = lax.optimization_barrier((block, w_gate[0], w_up[0], w_down[0]))
    packed = jnp.concatenate([gate, up, down.T], axis=1)
    weights = lax.all_gather(packed, "dp", axis=0, tiled=True)
    cores = [(i, i ^ 1) for i in range(nodes)]
    ring = [
        (n * places + z, n * places + (z + 1 - 2 * (n % 2)) % places)
        for n in range(nodes)
        for z in range(places)
    ]
    swap = lambda piece: lax.ppermute(piece, "node", cores)
    chains = list(lax.optimization_barrier((block, swap(block))))
    blocks, plan = list(chains), [(0, 0), (0, 1)]
    for hop in range(1, places // 2 + 1):
        for which in range(1 if 2 * hop == places else 2):
            chains[which] = lax.ppermute(chains[which], ("node", "local"), ring)
            blocks += [chains[which], swap(chains[which])]
            plan += [(hop, which), (-hop, 1 - which)]

    half = places * block.shape[0]
    vmem = pl.BlockSpec(memory_space=pltpu.VMEM)
    anywhere = pl.BlockSpec(memory_space=pl.ANY)
    grads, back, part = pl.pallas_call(
        functools.partial(gradients_kernel, plan),
        out_shape=(
            jax.ShapeDtypeStruct((3 * LANES, width), jnp.bfloat16),
            jax.ShapeDtypeStruct((2 * half, 2 * LANES), jnp.bfloat16),
            jax.ShapeDtypeStruct((2 * half, LANES), jnp.bfloat16),
        ),
        in_specs=[anywhere] * (1 + len(blocks)),
        out_specs=(anywhere, vmem, vmem),
        scratch_shapes=[
            pltpu.VMEM((2 * half, wide), jnp.bfloat16),
            pltpu.VMEM((width, 3 * LANES), jnp.bfloat16),
            pltpu.VMEM((3 * LANES, width), jnp.bfloat16),
            pltpu.SemaphoreType.DMA((4 * places + 1 + width // STEP,)),
        ],
        compiler_params=params(),
        name="gradients",
    )(weights, *blocks)

    share = lax.psum_scatter(grads, "dp", scatter_dimension=0, tiled=True)

    part_own, part_other = pl.pallas_call(
        input_kernel,
        out_shape=(
            jax.ShapeDtypeStruct((half, width + LANES), jnp.bfloat16),
            jax.ShapeDtypeStruct((half, width + LANES), jnp.bfloat16),
        ),
        in_specs=[vmem, vmem, vmem],
        out_specs=(vmem, vmem),
        compiler_params=params(),
        name="input_part",
    )(back, part, weights)
    arrived = lax.ppermute(part_other, "node", cores)
    chip = (part_own.astype(jnp.float32) + arrived.astype(jnp.float32)).astype(jnp.bfloat16)
    chip = chip.reshape(places, columns * count, width + LANES)
    cut = width // 2
    first = lax.all_to_all(chip[:, :, :cut], "local", 0, 0, tiled=True)
    share, first, rest = lax.optimization_barrier((share, first, chip[:, :, cut:]))
    summed = lax.all_gather(share, "dp", axis=0, tiled=True)
    rest = lax.all_to_all(rest, "local", 0, 0, tiled=True)
    column = jnp.concatenate(
        [jnp.sum(part.astype(jnp.float32), axis=0).astype(jnp.bfloat16) for part in (first, rest)],
        axis=1,
    )
    by_column = lax.all_to_all(
        column.reshape(columns, count, width + LANES),
        "node",
        0,
        0,
        tiled=True,
        axis_index_groups=same_core,
    )
    total = jnp.sum(by_column.astype(jnp.float32), axis=0)
    grad_tokens = total[:, :width].astype(jnp.bfloat16)
    grad_gates = jnp.sum(jnp.where(hits, total[:, None, width:], 0.0), axis=2).astype(jnp.bfloat16)

    grad_gate, grad_up, grad_down = pl.pallas_call(
        unpack_kernel,
        out_shape=(
            jax.ShapeDtypeStruct((1, width, LANES), jnp.bfloat16),
            jax.ShapeDtypeStruct((1, width, LANES), jnp.bfloat16),
            jax.ShapeDtypeStruct((1, LANES, width), jnp.bfloat16),
        ),
        in_specs=[anywhere],
        out_specs=(anywhere, anywhere, anywhere),
        scratch_shapes=[
            pltpu.VMEM((3 * LANES, width), jnp.bfloat16),
            pltpu.VMEM((2, width, LANES), jnp.bfloat16),
            pltpu.SemaphoreType.DMA((6,)),
        ],
        compiler_params=params(),
        name="unpack",
    )(summed)
    return grad_tokens, grad_gates, grad_gate, grad_up, grad_down


def solution(mesh):
    placed = (
        P(("dp", "node", "local"), None),
        P(("dp", "node", "local"), None),
        P(("dp", "node", "local"), None),
        P(("dp", "node", "local"), None),
        P("node", "dp", "local"),
        P("node", "dp", "local"),
        P("node", "local", "dp"),
    )
    return jax.shard_map(
        shards,
        mesh=mesh,
        in_specs=placed,
        out_specs=(
            P(("dp", "node", "local"), None),
            P(("dp", "node", "local"), None),
            P("node", None, "local"),
            P("node", None, "local"),
            P("node", "local", None),
        ),
        check_vma=False,
    )
```

```python
import functools

import jax
import jax.numpy as jnp
from jax import lax
from jax.experimental import pallas as pl
from jax.experimental.pallas import tpu as pltpu
from jax.sharding import PartitionSpec as P

LANES = 128
STEP = 1792


def gradients_kernel(plan, w_hbm, *refs):
    blocks = refs[: len(plan)]
    grads_hbm, back_ref, part_ref, rows, weights, grads, sems = refs[len(plan) :]
    half = rows.shape[0] // 2
    width = (rows.shape[1] - LANES) // 2
    node = lax.axis_index("node")
    here, towards = lax.axis_index("local"), 2 * lax.rem(node, 2) - 1
    size = blocks[0].shape[0]
    places = half // size
    early = [pltpu.make_async_copy(w_hbm, weights, sems.at[0])]
    late = []
    for source, (hop, which) in zip(blocks, plan):
        slot = lax.rem(here + towards * hop + places, places)
        target = rows.at[pl.ds(pl.multiple_of(which * half + slot * size, size), size)]
        count = len(early)
        for group, first, columns in ((early, 0, width), (late, width, width + LANES)):
            group.append(
                pltpu.make_async_copy(
                    source.at[:, pl.ds(first, columns)],
                    target.at[:, pl.ds(first, columns)],
                    sems.at[count + (2 * places if first else 0)],
                )
            )
    for copy in early + late:
        copy.start()
    for copy in early:
        copy.wait()

    def project(step, total):
        span = pl.ds(pl.multiple_of(step * STEP, STEP), STEP)
        return total + jnp.dot(
            rows[:, span], weights[span, : 2 * LANES], preferred_element_type=jnp.float32
        )

    def project_back(step, total):
        span = pl.ds(pl.multiple_of(step * STEP, STEP), STEP)
        shifted = pl.ds(pl.multiple_of(width + step * STEP, STEP), STEP)
        return total + jnp.dot(
            rows[:, shifted], weights[span, 2 * LANES :], preferred_element_type=jnp.float32
        )

    steps = width // STEP
    pre = lax.fori_loop(0, steps, project, jnp.zeros((2 * half, 2 * LANES), jnp.float32))
    for copy in late:
        copy.wait()
    raw = lax.fori_loop(0, steps, project_back, jnp.zeros((2 * half, LANES), jnp.float32))
    pre_gate, pre_up = pre[:, :LANES], pre[:, LANES:]
    lanes = lax.broadcasted_iota(jnp.int32, (1, LANES), 1)
    sel = (lanes == node).astype(jnp.float32)
    weight = jnp.sum(rows[:, 2 * width :].astype(jnp.float32) * sel, axis=1, keepdims=True)
    sigmoid = jax.nn.sigmoid(pre_gate)
    activated = (pre_gate * sigmoid * pre_up).astype(jnp.bfloat16).astype(jnp.float32)
    part_ref[...] = (jnp.sum(activated * raw, axis=1, keepdims=True) * sel).astype(jnp.bfloat16)
    grad_act = raw * weight
    back_gate = grad_act * pre_up * sigmoid * (1.0 + pre_gate * (1.0 - sigmoid))
    back_up = grad_act * pre_gate * sigmoid
    back = jnp.concatenate([back_gate, back_up], axis=1)
    back_ref[...] = back.astype(jnp.bfloat16)
    back_t = back.T.astype(jnp.bfloat16)
    activated_t = (activated * weight).T.astype(jnp.bfloat16)

    outgoing = []
    for step in range(steps):
        span = pl.ds(step * STEP, STEP)
        grads[: 2 * LANES, span] = jnp.dot(
            back_t, rows[:, span], preferred_element_type=jnp.float32
        ).astype(jnp.bfloat16)
        grads[2 * LANES :, span] = jnp.dot(
            activated_t,
            rows[:, pl.ds(width + step * STEP, STEP)],
            preferred_element_type=jnp.float32,
        ).astype(jnp.bfloat16)
        outgoing.append(
            pltpu.make_async_copy(
                grads.at[:, span], grads_hbm.at[:, span], sems.at[4 * places + 1 + step]
            )
        )
        outgoing[-1].start()
    for copy in outgoing:
        copy.wait()


def input_kernel(back_ref, part_ref, w_ref, own_ref, other_ref):
    half = own_ref.shape[0]
    width = own_ref.shape[1] - LANES

    def step_of(step, carry):
        span = pl.ds(pl.multiple_of(step * STEP, STEP), STEP)
        out = lax.dot_general(
            back_ref[...],
            w_ref[span, : 2 * LANES],
            (((1,), (1,)), ((), ())),
            preferred_element_type=jnp.float32,
        ).astype(jnp.bfloat16)
        own_ref[:, span] = out[:half]
        other_ref[:, span] = out[half:]
        return carry

    lax.fori_loop(0, width // STEP, step_of, 0)
    own_ref[:, width:] = part_ref[:half]
    other_ref[:, width:] = part_ref[half:]


def unpack_kernel(sum_hbm, gate_hbm, up_hbm, down_hbm, held, turned, sems):
    width = held.shape[1]
    tiles = [
        (n, target, pl.ds(first, STEP))
        for n, target in enumerate((gate_hbm, up_hbm))
        for first in range(0, width, STEP)
    ]
    total = len(tiles)
    arrivals = [
        pltpu.make_async_copy(
            sum_hbm.at[pl.ds(n * LANES, LANES), span],
            held.at[pl.ds(n * LANES, LANES), span],
            sems.at[k],
        )
        for k, (n, _, span) in enumerate(tiles)
    ]
    for copy in arrivals:
        copy.start()
    leaving = [
        pltpu.make_async_copy(
            sum_hbm.at[pl.ds(2 * LANES, LANES)], down_hbm.at[0], sems.at[2 * total]
        )
    ]
    leaving[0].start()
    for k, (n, target, span) in enumerate(tiles):
        arrivals[k].wait()
        turned[n, span, :] = (
            held[n * LANES : (n + 1) * LANES, span].astype(jnp.float32).T.astype(jnp.bfloat16)
        )
        leaving.append(
            pltpu.make_async_copy(turned.at[n, span], target.at[0, span], sems.at[total + k])
        )
        leaving[-1].start()
    for copy in leaving:
        copy.wait()


def params():
    return pltpu.CompilerParams(vmem_limit_bytes=60 * 1024 * 1024)


def shards(tokens, grad_out, router_gates, groups, w_gate, w_up, w_down):
    nodes = lax.axis_size("node")
    places = lax.axis_size("local")
    count, width = tokens.shape
    columns = nodes // 2
    wide = 2 * width + LANES

    lanes = jnp.arange(LANES, dtype=jnp.int32)
    hits = groups[:, :, None] == lanes[None, None, :]
    table = jnp.sum(
        jnp.where(hits, router_gates.astype(jnp.float32)[:, :, None], 0.0), axis=1
    ).astype(jnp.bfloat16)
    mine = jnp.concatenate([tokens, grad_out, table], axis=1)
    same_core = [[2 * x + core for x in range(columns)] for core in range(2)]
    block = lax.all_to_all(
        jnp.broadcast_to(mine, (columns, count, wide)),
        "node",
        0,
        0,
        tiled=True,
        axis_index_groups=same_core,
    ).reshape(columns * count, wide)
    block, gate, up, down = lax.optimization_barrier((block, w_gate[0], w_up[0], w_down[0]))
    packed = jnp.concatenate([gate, up, down.T], axis=1)
    weights = lax.all_gather(packed, "dp", axis=0, tiled=True)
    cores = [(i, i ^ 1) for i in range(nodes)]
    ring = [
        (n * places + z, n * places + (z + 1 - 2 * (n % 2)) % places)
        for n in range(nodes)
        for z in range(places)
    ]
    swap = lambda piece: lax.ppermute(piece, "node", cores)
    chains = list(lax.optimization_barrier((block, swap(block))))
    blocks, plan = list(chains), [(0, 0), (0, 1)]
    for hop in range(1, places // 2 + 1):
        for which in range(1 if 2 * hop == places else 2):
            chains[which] = lax.ppermute(chains[which], ("node", "local"), ring)
            blocks += [chains[which], swap(chains[which])]
            plan += [(hop, which), (-hop, 1 - which)]

    half = places * block.shape[0]
    vmem = pl.BlockSpec(memory_space=pltpu.VMEM)
    anywhere = pl.BlockSpec(memory_space=pl.ANY)
    grads, back, part = pl.pallas_call(
        functools.partial(gradients_kernel, plan),
        out_shape=(
            jax.ShapeDtypeStruct((3 * LANES, width), jnp.bfloat16),
            jax.ShapeDtypeStruct((2 * half, 2 * LANES), jnp.bfloat16),
            jax.ShapeDtypeStruct((2 * half, LANES), jnp.bfloat16),
        ),
        in_specs=[anywhere] * (1 + len(blocks)),
        out_specs=(anywhere, vmem, vmem),
        scratch_shapes=[
            pltpu.VMEM((2 * half, wide), jnp.bfloat16),
            pltpu.VMEM((width, 3 * LANES), jnp.bfloat16),
            pltpu.VMEM((3 * LANES, width), jnp.bfloat16),
            pltpu.SemaphoreType.DMA((4 * places + 1 + width // STEP,)),
        ],
        compiler_params=params(),
        name="gradients",
    )(weights, *blocks)

    share = lax.psum_scatter(grads, "dp", scatter_dimension=0, tiled=True)

    part_own, part_other = pl.pallas_call(
        input_kernel,
        out_shape=(
            jax.ShapeDtypeStruct((half, width + LANES), jnp.bfloat16),
            jax.ShapeDtypeStruct((half, width + LANES), jnp.bfloat16),
        ),
        in_specs=[vmem, vmem, vmem],
        out_specs=(vmem, vmem),
        compiler_params=params(),
        name="input_part",
    )(back, part, weights)
    arrived = lax.ppermute(part_other, "node", cores)
    chip = (part_own.astype(jnp.float32) + arrived.astype(jnp.float32)).astype(jnp.bfloat16)
    chip = chip.reshape(places, columns * count, width + LANES)
    cut = width // 2
    first = lax.all_to_all(chip[:, :, :cut], "local", 0, 0, tiled=True)
    share, first, rest = lax.optimization_barrier((share, first, chip[:, :, cut:]))
    summed = lax.all_gather(share, "dp", axis=0, tiled=True)
    rest = lax.all_to_all(rest, "local", 0, 0, tiled=True)
    column = jnp.concatenate(
        [jnp.sum(part.astype(jnp.float32), axis=0).astype(jnp.bfloat16) for part in (first, rest)],
        axis=1,
    )
    by_column = lax.all_to_all(
        column.reshape(columns, count, width + LANES),
        "node",
        0,
        0,
        tiled=True,
        axis_index_groups=same_core,
    )
    total = jnp.sum(by_column.astype(jnp.float32), axis=0)
    grad_tokens = total[:, :width].astype(jnp.bfloat16)
    grad_gates = jnp.sum(jnp.where(hits, total[:, None, width:], 0.0), axis=2).astype(jnp.bfloat16)

    grad_gate, grad_up, grad_down = pl.pallas_call(
        unpack_kernel,
        out_shape=(
            jax.ShapeDtypeStruct((1, width, LANES), jnp.bfloat16),
            jax.ShapeDtypeStruct((1, width, LANES), jnp.bfloat16),
            jax.ShapeDtypeStruct((1, LANES, width), jnp.bfloat16),
        ),
        in_specs=[anywhere],
        out_specs=(anywhere, anywhere, anywhere),
        scratch_shapes=[
            pltpu.VMEM((2 * LANES, width), jnp.bfloat16),
            pltpu.VMEM((2, width, LANES), jnp.bfloat16),
            pltpu.SemaphoreType.DMA((4 * width // STEP + 1,)),
        ],
        compiler_params=params(),
        name="unpack",
    )(summed)
    return grad_tokens, grad_gates, grad_gate, grad_up, grad_down


def solution(mesh):
    placed = (
        P(("dp", "node", "local"), None),
        P(("dp", "node", "local"), None),
        P(("dp", "node", "local"), None),
        P(("dp", "node", "local"), None),
        P("node", "dp", "local"),
        P("node", "dp", "local"),
        P("node", "local", "dp"),
    )
    return jax.shard_map(
        shards,
        mesh=mesh,
        in_specs=placed,
        out_specs=(
            P(("dp", "node", "local"), None),
            P(("dp", "node", "local"), None),
            P("node", None, "local"),
            P("node", None, "local"),
            P("node", "local", None),
        ),
        check_vma=False,
    )
```
